32 devices in a mesh: gx: 16 (over z, y, core), gy: 2 (over x).
Axes of the slice: x: 2, y: 2, z: 4, core: 2. Of those that a mesh axis runs over, the one named last changes fastest.
Arguments:
- state: bfloat16 [4, 2, 4096, 4096], P(None, None, 'gx', 'gy'), may hold values from -6 to 6
- heights: int32 [4096, 4096], P('gx', 'gy'), may hold values from 0 to 1
- surface_flag: int32 [4096, 4096], P('gx', 'gy'), may hold values 0 or 1
Outputs:
- tendency: bfloat16 [4, 2, 4096, 4096], P(None, None, 'gx', 'gy')
- spectrum: float32 [2, 2, 4096, 4096], P(None, None, ('gx', 'gy'))
The draws below stay inside these ranges and needn't reach their ends.
All inputs are finite; a program needn't handle non-finite values. No bound on the sum of `surface_flag` on one device may be relied on, other than what follows from the above.
Results may differ from the reference program's by a relative error of at most 0.002.
Values may be sent and summed in bfloat16 or wider, within the bound.
A program may use at most 192 MiB of HBM per device.

```python
import jax
import jax.numpy as jnp
from jax import lax

NX = 4096
NY = 4096
NZ = 2


def with_ends(values, own_key, smallest, top_value):
    longest = values.shape.index(max(values.shape))
    spots = []
    for shift in (0, 1):
        where = [jax.random.randint(jax.random.fold_in(own_key, axis), (), 0, length) for axis, length in enumerate(values.shape)]
        where[longest] = (where[longest] + shift) % values.shape[longest]
        spots.append(tuple(where))
    return values.at[spots[0]].set(smallest).at[spots[1]].set(top_value)


def level_of(key, shape, cuts, smallest, top_value):
    loudness = 1.0
    for position, parts in cuts:
        steps = jax.random.uniform(jax.random.fold_in(jax.random.fold_in(key, 6), position), (parts,), jnp.float32, smallest / len(cuts), top_value / len(cuts))
        loudness = loudness * jnp.repeat(jnp.exp(steps), shape[position] // parts).reshape((-1,) + (1,) * (len(shape) - 1 - position))
    return loudness


def gaussian(stream_key, extent, scale, bound, split=(), kind=jnp.bfloat16):
    loudness = level_of(stream_key, extent, split, -0.22, 0.18) if split else 1.0
    values = jax.random.normal(stream_key, extent, jnp.float32) * scale * loudness
    return jnp.minimum(jnp.maximum(values, -bound), bound).astype(kind)


def setup_inputs(seed: int = 0) -> dict:
    key_list = jax.random.split(jax.random.key(seed), 4)
    state = gaussian(key_list[0], (4, NZ, NX, NY), 1.0, 6.0, ((2, 16), (3, 2)))
    heights = with_ends(jax.random.randint(key_list[1], (NX, NY), 0, NZ // 2 + 1), jax.random.fold_in(key_list[1], 1), 0, (NZ // 2 + 1) - 1).astype(jnp.int32)
    surface_flag = with_ends((jax.random.randint(key_list[2], (NX, NY), 0, 2) < 1).astype(jnp.int32), jax.random.fold_in(key_list[2], 1), 0, 1)
    return {"state": state, "heights": heights, "surface_flag": surface_flag}


NU = 0.1
BETA = 0.5
HEAT = 1.0
DT = 0.5


def raised(field):
    zero = jnp.zeros_like(field[:1])
    return jnp.concatenate([field[1:], zero], axis=0)


def lowered(field):
    zero = jnp.zeros_like(field[:1])
    return jnp.concatenate([zero, field[:-1]], axis=0)


def tendency_one(component, field, pick, center, fluid, surface):
    slope_x = (45.0 * (pick(1, 0) - pick(-1, 0)) - 9.0 * (pick(2, 0) - pick(-2, 0)) + (pick(3, 0) - pick(-3, 0))) / 60.0
    slope_y = (45.0 * (pick(0, 1) - pick(0, -1)) - 9.0 * (pick(0, 2) - pick(0, -2)) + (pick(0, 3) - pick(0, -3))) / 60.0
    above = raised(field)
    below = lowered(field)
    slope_z = (above - below) * 0.5
    advect = center[0] * slope_x + center[1] * slope_y + center[2] * slope_z
    spread = (pick(1, 0) + pick(-1, 0) + pick(0, 1) + pick(0, -1) - 4.0 * field) + (above + below - 2.0 * field)
    result = NU * spread - advect
    if component == 2:
        result = result + BETA * center[3]
    if component == 3:
        result = result + HEAT * surface
    return fluid * result


def reference(state, heights, surface_flag):
    level = lax.broadcasted_iota(jnp.int32, state.shape[1:], 0)
    fluid = (level >= heights[None]).astype(jnp.float32)
    surface = (level == heights[None]).astype(jnp.float32) * surface_flag[None].astype(jnp.float32)
    masked = state.astype(jnp.float32) * fluid[None]
    pieces = []
    for component in range(4):
        field = masked[component]

        def pick(step_x, step_y, field=field):
            return jnp.roll(field, (-step_x, -step_y), axis=(1, 2))

        pieces.append(tendency_one(component, field, pick, masked, fluid, surface).astype(jnp.bfloat16))
    tendency = jnp.stack(pieces)
    star = masked[:3] + DT * tendency[:3].astype(jnp.float32)
    diverge = ((jnp.roll(star[0], -1, 1) - jnp.roll(star[0], 1, 1)) + (jnp.roll(star[1], -1, 2) - jnp.roll(star[1], 1, 2)) + (raised(star[2]) - lowered(star[2]))) * 0.5
    transformed = jnp.fft.fft2(diverge, axes=(1, 2), norm="ortho")
    transformed = jnp.transpose(transformed, (0, 2, 1))
    spectrum = jnp.stack([jnp.real(transformed), jnp.imag(transformed)]).astype(jnp.float32)
    return tendency, spectrum
```

```python
import functools
import math

import jax
import jax.numpy as jnp
import numpy as np
from jax import lax
from jax.experimental import pallas as pl
from jax.experimental.pallas import tpu as pltpu
from jax.sharding import PartitionSpec as P

NU = 0.1
BETA = 0.5
HEAT = 1.0
DT = 0.5
RADIX = 16
SEND = jnp.float16
BF = jnp.bfloat16
F32 = jnp.float32
SLOPE = {1: 45.0, -1: -45.0, 2: -9.0, -2: 9.0, 3: 1.0, -3: -1.0}
CURVE_X = {1: 1.0, -1: 1.0}
CURVE_Y = {0: -6.0, 1: 1.0, -1: 1.0}
CENTRAL = {1: 1.0, -1: -1.0}


def band(rows, columns, offset, taps):
    step = np.arange(rows)[:, None] - np.arange(columns)[None, :] - offset
    out = np.zeros((rows, columns), np.float32)
    for key, value in taps.items():
        out[step == key] = value
    return out


def dot(a, b):
    return jnp.dot(a, b, preferred_element_type=F32)


def dot_t(a, b):
    return lax.dot_general(a, b, (((1,), (1,)), ((), ())), preferred_element_type=F32)


def stencil_kernel(
    bx, width,
    main, prev, nxt, heights, h_prev, h_next, flag, xlo, xhi, yl, yr, dy, dx, sy, sx,
    tend, div0, div1,
    m_s, h_s, t_s,
):
    i = pl.program_id(0)
    last = pl.num_programs(0) - 1
    rows = bx + 16
    ext = width + 256
    mine = slice(8, 8 + bx)
    divs = (div0, div1)
    side = pl.ds(pl.multiple_of(i * bx, 16), rows)


    piece = 256

    def fill(c, carry):
        lanes = pl.ds(pl.multiple_of(c * piece, 128), piece)
        target = pl.ds(pl.multiple_of(128 + c * piece, 128), piece)

        def edge(field, ref_low, ref_high, middle):
            low = jnp.where(i == 0, xlo[field, :, lanes].astype(F32), ref_low)
            high = jnp.where(i == last, xhi[field, :, lanes].astype(F32), ref_high)
            return jnp.concatenate([low, middle, high], axis=0)

        h = edge(
            8, h_prev[:, lanes].astype(F32), h_next[:, lanes].astype(F32),
            heights[:, lanes].astype(F32),
        )
        h_s[:, target] = h
        for f in range(8):
            value = edge(
                f, prev[f // 2, f % 2, :, lanes].astype(F32)[8:],
                nxt[f // 2, f % 2, :, lanes].astype(F32)[:8],
                main[f // 2, f % 2, :, lanes].astype(F32),
            )
            m_s[f, :, target] = jnp.where(h <= float(f % 2), value, 0.0).astype(BF)
        return carry

    lax.fori_loop(0, width // piece, fill, 0)
    for ref, target in ((yl, slice(0, 128)), (yr, slice(width + 128, ext))):
        h = ref[8, side, :].astype(F32)
        h_s[:, target] = h
        for f in range(8):
            m_s[f, :, target] = jnp.where(
                h <= float(f % 2), ref[f, side, :].astype(F32), 0.0
            ).astype(BF)

    def tendency(f, lanes, window, matrix, centers, fluids, n):
        k = f % 2
        mid = m_s[f, :, lanes]
        along_y = dot(m_s[f, :, window], matrix)
        along_x = dot(dx[...], mid)
        other = m_s[f + 1 - 2 * k, :, lanes].astype(F32)
        u60, v60, wz = centers[k]
        lap = along_y[:, n:] + along_x[rows:] + other
        out = NU * lap - (u60 * along_x[:rows] + v60 * along_y[:, :n] + wz * other)
        return out

    def centers_of(lanes):
        out = []
        for k in range(2):
            sign = 0.5 if k == 0 else -0.5
            out.append((
                m_s[k, :, lanes].astype(F32) * (1.0 / 60.0),
                m_s[2 + k, :, lanes].astype(F32) * (1.0 / 60.0),
                m_s[4 + k, :, lanes].astype(F32) * sign,
            ))
        return out

    def first(j, carry):
        start = pl.multiple_of(j * 256, 128)
        lanes = pl.ds(pl.multiple_of(start + 128, 128), 256)
        window = pl.ds(start, 512)
        outs = pl.ds(start, 256)
        centers = centers_of(lanes)
        h = h_s[:, lanes]
        fluids = [(h <= float(k)).astype(F32) for k in range(2)]
        shine = flag[:, outs].astype(F32)
        stars = []
        for k in range(2):
            for c in (0, 1, 2, 3):
                f = 2 * c + k
                t = tendency(f, lanes, window, dy[...], centers, fluids, 256)
                if c == 2:
                    t = t + BETA * m_s[6 + k, :, lanes].astype(F32)
                if c == 3:
                    t = t[mine] + HEAT * jnp.where(h[mine] == float(k), shine, 0.0)
                    tend[c, k, :, outs] = (fluids[k][mine] * t).astype(BF)
                    continue
                t = fluids[k] * t
                tend[c, k, :, outs] = t[mine].astype(BF)
                if c == 0:
                    tb = t.astype(BF)
                    divs[k][:, outs] = dot(sx[0], m_s[f, :, lanes]) + dot(sx[1], tb)
                if c == 1:
                    t_s[k, :, lanes] = t.astype(BF)
                if c == 2:
                    tb = t[mine].astype(BF).astype(F32)
                    stars.append(m_s[f, :, lanes].astype(F32)[mine] + DT * tb)
        div0[:, outs] += stars[1]
        div1[:, outs] -= stars[0]
        return carry

    lax.fori_loop(0, width // 256, first, 0)

    for target, window, matrix in (
        (slice(0, 128), slice(0, 256),
         jnp.concatenate([dy[128:384, 0:128], dy[128:384, 256:384]], axis=1)),
        (slice(ext - 128, ext), slice(ext - 256, ext),
         jnp.concatenate([dy[0:256, 0:128], dy[0:256, 256:384]], axis=1)),
    ):
        centers = centers_of(target)
        h = h_s[:, target]
        for k in range(2):
            t = tendency(2 + k, target, window, matrix, centers, None, 128)
            t_s[k, :, target] = jnp.where(h <= float(k), t, 0.0).astype(BF)

    def second(j, carry):
        start = pl.multiple_of(j * 256, 128)
        window = pl.ds(start, 512)
        outs = pl.ds(start, 256)
        for k in range(2):
            part = dot(m_s[2 + k, :, window], sy[0]) + dot(t_s[k, :, window], sy[1])
            divs[k][:, outs] = (divs[k][:, outs] + part[mine]) * 0.5
        return carry

    lax.fori_loop(0, width // 256, second, 0)


def stencil(state, heights, flag, xlo, xhi, yl, yr):
    _, _, length, width = state.shape
    bx = min(128, length)
    rows = bx + 16
    ext = width + 256
    dy = np.concatenate([band(512, 256, 128, SLOPE), band(512, 256, 128, CURVE_Y)], axis=1)
    dx = np.concatenate([band(rows, rows, 0, SLOPE).T, band(rows, rows, 0, CURVE_X).T], axis=0)
    sy = band(512, 256, 128, CENTRAL)
    sy = np.stack([sy, DT * sy])
    sx = band(rows, bx, 8, CENTRAL).T
    sx = np.stack([sx, DT * sx])
    n16 = length // 16
    n8 = length // 8
    full = lambda *shape: pl.BlockSpec(shape, lambda i: (0,) * len(shape))
    return pl.pallas_call(
        functools.partial(stencil_kernel, bx, width),
        grid=(length // bx,),
        out_shape=(
            jax.ShapeDtypeStruct(state.shape, BF),
            jax.ShapeDtypeStruct((length, width), F32),
            jax.ShapeDtypeStruct((length, width), F32),
        ),
        in_specs=[
            pl.BlockSpec((4, 2, bx, width), lambda i: (0, 0, i, 0)),
            pl.BlockSpec((4, 2, 16, width), lambda i: (0, 0, jnp.maximum(i * (bx // 16) - 1, 0), 0)),
            pl.BlockSpec((4, 2, 16, width), lambda i: (0, 0, jnp.minimum((i + 1) * (bx // 16), n16 - 1), 0)),
            pl.BlockSpec((bx, width), lambda i: (i, 0)),
            pl.BlockSpec((8, width), lambda i: (jnp.maximum(i * (bx // 8) - 1, 0), 0)),
            pl.BlockSpec((8, width), lambda i: (jnp.minimum((i + 1) * (bx // 8), n8 - 1), 0)),
            pl.BlockSpec((bx, width), lambda i: (i, 0)),
            full(9, 8, width),
            full(9, 8, width),
            full(9, length + 16, 128),
            full(9, length + 16, 128),
            full(512, 512),
            full(2 * rows, rows),
            full(2, 512, 256),
            full(2, bx, rows),
        ],
        out_specs=(
            pl.BlockSpec((4, 2, bx, width), lambda i: (0, 0, i, 0)),
            pl.BlockSpec((bx, width), lambda i: (i, 0)),
            pl.BlockSpec((bx, width), lambda i: (i, 0)),
        ),
        scratch_shapes=[
            pltpu.VMEM((8, rows, ext), BF),
            pltpu.VMEM((rows, ext), F32),
            pltpu.VMEM((2, rows, ext), BF),
        ],
        compiler_params=pltpu.CompilerParams(vmem_limit_bytes=56 * 2**20),
        name="stencil",
    )(state, state, state, heights, heights, heights, flag, xlo, xhi, yl, yr,
      jnp.asarray(dy, BF), jnp.asarray(dx, BF), jnp.asarray(sy, BF), jnp.asarray(sx, BF))


def fft(values):
    n = len(values)
    if n == 1:
        return values
    even, odd = fft(values[0::2]), fft(values[1::2])
    out = [None] * n
    for k in range(n // 2):
        er, ei = even[k]
        pr, pi = rotate(odd[k], k, n)
        out[k] = (er + pr, ei + pi)
        out[k + n // 2] = (er - pr, ei - pi)
    return out


def rotate(value, k, n):
    re, im = value
    if k == 0:
        return re, im
    if 4 * k == n:
        return im, -re
    if 8 * k == n:
        root = math.sqrt(0.5)
        return (re + im) * root, (im - re) * root
    if 8 * k == 3 * n:
        root = math.sqrt(0.5)
        return (im - re) * root, -(re + im) * root
    c, s = math.cos(2 * math.pi * k / n), math.sin(2 * math.pi * k / n)
    return re * c + im * s, im * c - re * s


def rfft(values):
    n = len(values)
    if n == 2:
        a, b = values
        return [(a + b, None), (a - b, None)]
    even, odd = rfft(values[0::2]), rfft(values[1::2])
    half = n // 2

    def at(part, k):
        if k <= half // 2:
            return part[k]
        re, im = part[half - k]
        return re, None if im is None else -im

    out = []
    for k in range(half + 1):
        er, ei = at(even, k % half)
        orr, oi = at(odd, k % half)
        if k == half:
            out.append((er - orr, None))
        elif k == 0:
            out.append((er + orr, None))
        elif 4 * k == n:
            out.append((er, -orr))
        else:
            if oi is None:
                c, s = math.cos(2 * math.pi * k / n), math.sin(2 * math.pi * k / n)
                pr, pi = orr * c, -orr * s
            else:
                pr, pi = rotate((orr, oi), k, n)
            out.append((er + pr, pi if ei is None else ei + pi))
    return out


def split(value):
    high = value.astype(BF)
    return high, (value - high.astype(F32)).astype(BF)


def complex_matrix(angle, scale):
    c, s = np.cos(angle) * scale, np.sin(angle) * scale
    full = np.block([[c, s], [-s, c]])
    high = full.astype(np.float32).astype(jnp.bfloat16)
    low = (full - high.astype(np.float64)).astype(jnp.bfloat16)
    return np.stack([high, low])


def y_kernel(inner, groups, each, f, tw, w, out, hi, lo):
    sources, length, width = f.shape
    chunks = width // inner

    def strip(i, carry):
        r = pl.ds(pl.multiple_of(i * 16, 16), 16)
        for c in range(inner // 128):
            lane = slice(c * 128, c * 128 + 128)
            values = []
            for q in range(RADIX):
                s, o = q // chunks, (q % chunks) * inner + c * 128
                values.append(f[s, r, o : o + 128].astype(F32))
            spec = rfft(values)
            for t in range(RADIX):
                re, im = spec[t if t <= RADIX // 2 else RADIX - t]
                cos = tw[0, t : t + 1, lane]
                sin = tw[1, t : t + 1, lane]
                if im is None:
                    zr, zi = re * cos, -(re * sin)
                elif t <= RADIX // 2:
                    zr, zi = re * cos + im * sin, im * cos - re * sin
                else:
                    zr, zi = re * cos - im * sin, -(im * cos + re * sin)
                zrh, zrl = split(zr)
                zih, zil = split(zi)
                hi[t, r, lane] = zrh
                lo[t, r, lane] = zrl
                lane_i = slice(inner + c * 128, inner + c * 128 + 128)
                hi[t, r, lane_i] = zih
                lo[t, r, lane_i] = zil
        return carry

    lax.fori_loop(0, length // 16, strip, 0)

    def multiply(t, carry):
        h = hi[t]
        got = dot_t(w[0], h) + dot_t(w[0], lo[t]) + dot_t(w[1], h)
        for part in range(2):
            for g in range(groups):
                base = (part * groups + g) * each
                for c in range(length // 128):
                    out[g, part, c, pl.ds(t, each, stride=RADIX), :] = got[
                        base : base + each, c * 128 : c * 128 + 128
                    ]
        return carry

    lax.fori_loop(0, RADIX, multiply, 0)


def transform_y(f, twiddle, matrix, groups, each):
    sources, length, width = f.shape
    inner = sources * width // RADIX
    return pl.pallas_call(
        functools.partial(y_kernel, inner, groups, each),
        out_shape=jax.ShapeDtypeStruct((groups, 2, length // 128, each * RADIX, 128), F32),
        in_specs=[pl.BlockSpec(memory_space=pltpu.VMEM)] * 3,
        out_specs=pl.BlockSpec(memory_space=pltpu.VMEM),
        scratch_shapes=[
            pltpu.VMEM((RADIX, length, 2 * inner), BF),
            pltpu.VMEM((RADIX, length, 2 * inner), BF),
        ],
        compiler_params=pltpu.CompilerParams(vmem_limit_bytes=56 * 2**20),
        cost_estimate=pl.CostEstimate(flops=10**10, bytes_accessed=10**7, transcendentals=0),
        name="transform_y",
    )(f, twiddle, matrix)


def x_kernel(z, tw, v, out, hi, lo, wide):
    count, _, pieces, waves, lanes_each = z.shape
    length = pieces * lanes_each
    inner = wide.shape[1] // count

    def strip(i, carry):
        r = pl.ds(pl.multiple_of(i * 16, 16), 16)
        for c in range(pieces):
            lane = slice(c * lanes_each, (c + 1) * lanes_each)
            values = [(z[a, 0, c, r, :].astype(F32), z[a, 1, c, r, :].astype(F32)) for a in range(count)]
            for t, (re, im) in enumerate(fft(values)):
                cos = tw[0, t : t + 1, lane]
                sin = tw[1, t : t + 1, lane]
                zrh, zrl = split(re * cos + im * sin)
                zih, zil = split(im * cos - re * sin)
                hi[t, r, lane] = zrh
                lo[t, r, lane] = zrl
                lane_i = slice(length + c * lanes_each, length + (c + 1) * lanes_each)
                hi[t, r, lane_i] = zih
                lo[t, r, lane_i] = zil
        return carry

    lax.fori_loop(0, waves // 16, strip, 0)

    def multiply(t, carry):
        h = hi[t]
        got = dot_t(v[0], h) + dot_t(v[0], lo[t]) + dot_t(v[1], h)
        for part in range(2):
            wide[part, pl.ds(t, inner, stride=count), :] = got[part * inner : (part + 1) * inner]
        return carry

    lax.fori_loop(0, count, multiply, 0)

    def turn(c, carry):
        block = pl.ds(pl.multiple_of(c * 256, 256), 256)
        for part in range(2):
            out[part, :, block] = wide[part, block, :].T[: out.shape[1]]
        return carry

    lax.fori_loop(0, wide.shape[1] // 256, turn, 0)


def transform_x(z, twiddle, matrix):
    count, _, pieces, waves, lanes_each = z.shape
    length = pieces * lanes_each
    total = count * length
    padded = max(waves, 128)
    return pl.pallas_call(
        x_kernel,
        out_shape=jax.ShapeDtypeStruct((2, waves, total), F32),
        in_specs=[pl.BlockSpec(memory_space=pltpu.VMEM)] * 3,
        out_specs=pl.BlockSpec(memory_space=pltpu.VMEM),
        scratch_shapes=[
            pltpu.VMEM((count, padded, 2 * length), BF),
            pltpu.VMEM((count, padded, 2 * length), BF),
            pltpu.VMEM((2, total, padded), F32),
        ],
        compiler_params=pltpu.CompilerParams(vmem_limit_bytes=56 * 2**20),
        cost_estimate=pl.CostEstimate(flops=10**10, bytes_accessed=10**7, transcendentals=0),
        name="transform_x",
    )(z, twiddle, matrix)


def tables(count_x, count_y, length, width):
    total_x, total_y = count_x * length, count_y * width
    inner = total_y // RADIX
    waves = total_y // (count_x * count_y)
    each = waves // RADIX
    p = np.arange(inner)
    shift = np.arange(RADIX)[None, :, None] + waves * np.arange(count_y)[:, None, None]
    angle = 2 * np.pi * ((shift * p) % total_y) / total_y
    tw_y = np.stack([np.cos(angle), np.sin(angle)], axis=1).astype(np.float32)
    m = ((np.arange(count_x) * count_y * each)[:, None] + np.arange(each)[None, :]).reshape(-1)
    w = complex_matrix(2 * np.pi * ((m[:, None] * p[None, :]) % inner) / inner, 1 / math.sqrt(total_y))
    l = np.arange(length)
    angle = 2 * np.pi * ((np.arange(count_x)[:, None] * l[None, :]) % total_x) / total_x
    tw_x = np.stack([np.cos(angle), np.sin(angle)]).astype(np.float32)
    v = complex_matrix(2 * np.pi * ((l[:, None] * l[None, :]) % length) / length, 1 / math.sqrt(total_x))
    return tw_y, w, tw_x, v, each


def around(axis, first, final):
    count = lax.axis_size(axis)
    up = [(i, (i + 1) % count) for i in range(count)]
    down = [(j, i) for i, j in up]
    return lax.ppermute(final, axis, up), lax.ppermute(first, axis, down)


def body(state, heights, flag):
    _, levels, length, width = state.shape
    count_x, count_y = lax.axis_size("gx"), lax.axis_size("gy")
    tw_y, w, tw_x, v, each = tables(count_x, count_y, length, width)

    def pieces(lo, hi, axis):
        s = lax.slice_in_dim(state, lo, hi, axis=axis + 2)
        s = s.reshape((8,) + s.shape[2:])
        return jnp.concatenate([s, lax.slice_in_dim(heights, lo, hi, axis=axis)[None].astype(BF)], axis=0)

    xlo, xhi = around("gx", pieces(0, 8, 0), pieces(length - 8, length, 0))
    left = jnp.concatenate([xlo[:, :, :4], pieces(0, 4, 1), xhi[:, :, :4]], axis=1)
    right = jnp.concatenate(
        [xlo[:, :, width - 4 :], pieces(width - 4, width, 1), xhi[:, :, width - 4 :]], axis=1
    )
    before, after = around("gy", left, right)
    yl = jnp.pad(before, ((0, 0), (0, 0), (124, 0)))
    yr = jnp.pad(after, ((0, 0), (0, 0), (0, 124)))
    tendency, div0, div1 = stencil(state, heights, flag, xlo, xhi, yl, yr)

    mine = lax.axis_index("gy")
    twiddle = lax.dynamic_index_in_dim(jnp.asarray(tw_y), mine, 0, keepdims=False)
    results = []
    for div in (div0, div1):
        lines = lax.all_gather(div.astype(SEND), "gy", axis=0).astype(F32)
        waves = transform_y(lines, twiddle, jnp.asarray(w), count_x, each)
        moved = lax.all_to_all(waves.astype(SEND), "gx", split_axis=0, concat_axis=0, tiled=True)
        results.append(transform_x(moved.astype(F32), jnp.asarray(tw_x), jnp.asarray(v)))
    return tendency, jnp.stack(results, axis=1)


def solution(mesh):
    return jax.shard_map(
        body,
        mesh=mesh,
        in_specs=(P(None, None, "gx", "gy"), P("gx", "gy"), P("gx", "gy")),
        out_specs=(P(None, None, "gx", "gy"), P(None, None, ("gx", "gy"), None)),
        check_vma=False,
    )
```

```python
import functools
import math

import jax
import jax.numpy as jnp
import numpy as np
from jax import lax
from jax.experimental import pallas as pl
from jax.experimental.pallas import tpu as pltpu
from jax.sharding import PartitionSpec as P

NU = 0.1
BETA = 0.5
HEAT = 1.0
DT = 0.5
RADIX = 16
SEND = jnp.float16
BF = jnp.bfloat16
F32 = jnp.float32
SLOPE = {1: 45.0, -1: -45.0, 2: -9.0, -2: 9.0, 3: 1.0, -3: -1.0}
CURVE_X = {1: 1.0, -1: 1.0}
CURVE_Y = {0: -6.0, 1: 1.0, -1: 1.0}
CENTRAL = {1: 1.0, -1: -1.0}


def band(rows, columns, offset, taps):
    step = np.arange(rows)[:, None] - np.arange(columns)[None, :] - offset
    out = np.zeros((rows, columns), np.float32)
    for key, value in taps.items():
        out[step == key] = value
    return out


def dot(a, b):
    return jnp.dot(a, b, preferred_element_type=F32)


def dot_t(a, b):
    return lax.dot_general(a, b, (((1,), (1,)), ((), ())), preferred_element_type=F32)


def stencil_kernel(
    bx, width,
    main, prev, nxt, heights, h_prev, h_next, flag, xlo, xhi, yl, yr, dy, dx, sy, sx,
    tend, div0, div1,
    m_s, h_s, t_s,
):
    i = pl.program_id(0)
    last = pl.num_programs(0) - 1
    rows = bx + 16
    ext = width + 256
    mine = slice(8, 8 + bx)
    divs = (div0, div1)
    side = pl.ds(pl.multiple_of(i * bx, 16), rows)


    piece = 256

    def fill(c, carry):
        lanes = pl.ds(pl.multiple_of(c * piece, 128), piece)
        target = pl.ds(pl.multiple_of(128 + c * piece, 128), piece)

        def edge(field, ref_low, ref_high, middle):
            low = jnp.where(i == 0, xlo[field, :, lanes].astype(F32), ref_low)
            high = jnp.where(i == last, xhi[field, :, lanes].astype(F32), ref_high)
            return jnp.concatenate([low, middle, high], axis=0)

        h = edge(
            8, h_prev[:, lanes].astype(F32), h_next[:, lanes].astype(F32),
            heights[:, lanes].astype(F32),
        )
        h_s[:, target] = h
        for f in range(8):
            value = edge(
                f, prev[f // 2, f % 2, :, lanes].astype(F32)[8:],
                nxt[f // 2, f % 2, :, lanes].astype(F32)[:8],
                main[f // 2, f % 2, :, lanes].astype(F32),
            )
            m_s[f, :, target] = jnp.where(h <= float(f % 2), value, 0.0).astype(BF)
        return carry

    lax.fori_loop(0, width // piece, fill, 0)
    for ref, target in ((yl, slice(0, 128)), (yr, slice(width + 128, ext))):
        h = ref[8, side, :].astype(F32)
        h_s[:, target] = h
        for f in range(8):
            m_s[f, :, target] = jnp.where(
                h <= float(f % 2), ref[f, side, :].astype(F32), 0.0
            ).astype(BF)

    def tendency(f, lanes, window, matrix, centers, fluids, n):
        k = f % 2
        mid = m_s[f, :, lanes]
        along_y = dot(m_s[f, :, window], matrix)
        along_x = dot(dx[...], mid)
        other = m_s[f + 1 - 2 * k, :, lanes].astype(F32)
        u60, v60, wz = centers[k]
        lap = along_y[:, n:] + along_x[rows:] + other
        out = NU * lap - (u60 * along_x[:rows] + v60 * along_y[:, :n] + wz * other)
        return out

    def centers_of(lanes):
        out = []
        for k in range(2):
            sign = 0.5 if k == 0 else -0.5
            out.append((
                m_s[k, :, lanes].astype(F32) * (1.0 / 60.0),
                m_s[2 + k, :, lanes].astype(F32) * (1.0 / 60.0),
                m_s[4 + k, :, lanes].astype(F32) * sign,
            ))
        return out

    def first(j, carry):
        start = pl.multiple_of(j * 256, 128)
        lanes = pl.ds(pl.multiple_of(start + 128, 128), 256)
        window = pl.ds(start, 512)
        outs = pl.ds(start, 256)
        centers = centers_of(lanes)
        h = h_s[:, lanes]
        fluids = [(h <= float(k)).astype(F32) for k in range(2)]
        shine = flag[:, outs].astype(F32)
        stars = []
        for k in range(2):
            for c in (0, 1, 2, 3):
                f = 2 * c + k
                t = tendency(f, lanes, window, dy[...], centers, fluids, 256)
                if c == 2:
                    t = t + BETA * m_s[6 + k, :, lanes].astype(F32)
                if c == 3:
                    t = t[mine] + HEAT * jnp.where(h[mine] == float(k), shine, 0.0)
                    tend[c, k, :, outs] = (fluids[k][mine] * t).astype(BF)
                    continue
                t = fluids[k] * t
                tend[c, k, :, outs] = t[mine].astype(BF)
                if c == 0:
                    tb = t.astype(BF)
                    divs[k][:, outs] = dot(sx[0], m_s[f, :, lanes]) + dot(sx[1], tb)
                if c == 1:
                    t_s[k, :, lanes] = t.astype(BF)
                if c == 2:
                    tb = t[mine].astype(BF).astype(F32)
                    stars.append(m_s[f, :, lanes].astype(F32)[mine] + DT * tb)
        div0[:, outs] += stars[1]
        div1[:, outs] -= stars[0]
        return carry

    lax.fori_loop(0, width // 256, first, 0)

    for target, window, matrix in (
        (slice(0, 128), slice(0, 256),
         jnp.concatenate([dy[128:384, 0:128], dy[128:384, 256:384]], axis=1)),
        (slice(ext - 128, ext), slice(ext - 256, ext),
         jnp.concatenate([dy[0:256, 0:128], dy[0:256, 256:384]], axis=1)),
    ):
        centers = centers_of(target)
        h = h_s[:, target]
        for k in range(2):
            t = tendency(2 + k, target, window, matrix, centers, None, 128)
            t_s[k, :, target] = jnp.where(h <= float(k), t, 0.0).astype(BF)

    def second(j, carry):
        start = pl.multiple_of(j * 256, 128)
        window = pl.ds(start, 512)
        outs = pl.ds(start, 256)
        for k in range(2):
            part = dot(m_s[2 + k, :, window], sy[0]) + dot(t_s[k, :, window], sy[1])
            divs[k][:, outs] = (divs[k][:, outs] + part[mine]) * 0.5
        return carry

    lax.fori_loop(0, width // 256, second, 0)


def stencil(state, heights, flag, xlo, xhi, yl, yr):
    _, _, length, width = state.shape
    bx = min(128, length)
    rows = bx + 16
    ext = width + 256
    dy = np.concatenate([band(512, 256, 128, SLOPE), band(512, 256, 128, CURVE_Y)], axis=1)
    dx = np.concatenate([band(rows, rows, 0, SLOPE).T, band(rows, rows, 0, CURVE_X).T], axis=0)
    sy = band(512, 256, 128, CENTRAL)
    sy = np.stack([sy, DT * sy])
    sx = band(rows, bx, 8, CENTRAL).T
    sx = np.stack([sx, DT * sx])
    n16 = length // 16
    n8 = length // 8
    full = lambda *shape: pl.BlockSpec(shape, lambda i: (0,) * len(shape))
    return pl.pallas_call(
        functools.partial(stencil_kernel, bx, width),
        grid=(length // bx,),
        out_shape=(
            jax.ShapeDtypeStruct(state.shape, BF),
            jax.ShapeDtypeStruct((length, width), F32),
            jax.ShapeDtypeStruct((length, width), F32),
        ),
        in_specs=[
            pl.BlockSpec((4, 2, bx, width), lambda i: (0, 0, i, 0)),
            pl.BlockSpec((4, 2, 16, width), lambda i: (0, 0, jnp.maximum(i * (bx // 16) - 1, 0), 0)),
            pl.BlockSpec((4, 2, 16, width), lambda i: (0, 0, jnp.minimum((i + 1) * (bx // 16), n16 - 1), 0)),
            pl.BlockSpec((bx, width), lambda i: (i, 0)),
            pl.BlockSpec((8, width), lambda i: (jnp.maximum(i * (bx // 8) - 1, 0), 0)),
            pl.BlockSpec((8, width), lambda i: (jnp.minimum((i + 1) * (bx // 8), n8 - 1), 0)),
            pl.BlockSpec((bx, width), lambda i: (i, 0)),
            full(9, 8, width),
            full(9, 8, width),
            full(9, length + 16, 128),
            full(9, length + 16, 128),
            full(512, 512),
            full(2 * rows, rows),
            full(2, 512, 256),
            full(2, bx, rows),
        ],
        out_specs=(
            pl.BlockSpec((4, 2, bx, width), lambda i: (0, 0, i, 0)),
            pl.BlockSpec((bx, width), lambda i: (i, 0)),
            pl.BlockSpec((bx, width), lambda i: (i, 0)),
        ),
        scratch_shapes=[
            pltpu.VMEM((8, rows, ext), BF),
            pltpu.VMEM((rows, ext), F32),
            pltpu.VMEM((2, rows, ext), BF),
        ],
        compiler_params=pltpu.CompilerParams(vmem_limit_bytes=56 * 2**20),
        name="stencil",
    )(state, state, state, heights, heights, heights, flag, xlo, xhi, yl, yr,
      jnp.asarray(dy, BF), jnp.asarray(dx, BF), jnp.asarray(sy, BF), jnp.asarray(sx, BF))


def fft(values):
    n = len(values)
    if n == 1:
        return values
    even, odd = fft(values[0::2]), fft(values[1::2])
    out = [None] * n
    for k in range(n // 2):
        er, ei = even[k]
        pr, pi = rotate(odd[k], k, n)
        out[k] = (er + pr, ei + pi)
        out[k + n // 2] = (er - pr, ei - pi)
    return out


def rotate(value, k, n):
    re, im = value
    if k == 0:
        return re, im
    if 4 * k == n:
        return im, -re
    if 8 * k == n:
        root = math.sqrt(0.5)
        return (re + im) * root, (im - re) * root
    if 8 * k == 3 * n:
        root = math.sqrt(0.5)
        return (im - re) * root, -(re + im) * root
    c, s = math.cos(2 * math.pi * k / n), math.sin(2 * math.pi * k / n)
    return re * c + im * s, im * c - re * s


def rfft(values):
    n = len(values)
    if n == 2:
        a, b = values
        return [(a + b, None), (a - b, None)]
    even, odd = rfft(values[0::2]), rfft(values[1::2])
    half = n // 2

    def at(part, k):
        if k <= half // 2:
            return part[k]
        re, im = part[half - k]
        return re, None if im is None else -im

    out = []
    for k in range(half + 1):
        er, ei = at(even, k % half)
        orr, oi = at(odd, k % half)
        if k == half:
            out.append((er - orr, None))
        elif k == 0:
            out.append((er + orr, None))
        elif 4 * k == n:
            out.append((er, -orr))
        else:
            if oi is None:
                c, s = math.cos(2 * math.pi * k / n), math.sin(2 * math.pi * k / n)
                pr, pi = orr * c, -orr * s
            else:
                pr, pi = rotate((orr, oi), k, n)
            out.append((er + pr, pi if ei is None else ei + pi))
    return out


def split(value):
    high = value.astype(BF)
    return high, (value - high.astype(F32)).astype(BF)


def complex_matrix(angle, scale):
    c, s = np.cos(angle) * scale, np.sin(angle) * scale
    full = np.block([[c, s], [-s, c]])
    high = full.astype(np.float32).astype(jnp.bfloat16)
    low = (full - high.astype(np.float64)).astype(jnp.bfloat16)
    return np.stack([high, low])


def y_kernel(inner, groups, each, f, tw, w, out, hi, lo):
    sources, length, width = f.shape
    chunks = width // inner

    def strip(i, carry):
        r = pl.ds(pl.multiple_of(i * 16, 16), 16)
        for c in range(inner // 128):
            lane = slice(c * 128, c * 128 + 128)
            values = []
            for q in range(RADIX):
                s, o = q // chunks, (q % chunks) * inner + c * 128
                values.append(f[s, r, o : o + 128].astype(F32))
            spec = rfft(values)
            for t in range(RADIX):
                re, im = spec[t if t <= RADIX // 2 else RADIX - t]
                cos = tw[0, t : t + 1, lane]
                sin = tw[1, t : t + 1, lane]
                if im is None:
                    zr, zi = re * cos, -(re * sin)
                elif t <= RADIX // 2:
                    zr, zi = re * cos + im * sin, im * cos - re * sin
                else:
                    zr, zi = re * cos - im * sin, -(im * cos + re * sin)
                zrh, zrl = split(zr)
                zih, zil = split(zi)
                hi[t, r, lane] = zrh
                lo[t, r, lane] = zrl
                lane_i = slice(inner + c * 128, inner + c * 128 + 128)
                hi[t, r, lane_i] = zih
                lo[t, r, lane_i] = zil
        return carry

    lax.fori_loop(0, length // 16, strip, 0)

    def multiply(t, carry):
        h = hi[t]
        got = dot_t(w[0], h) + dot_t(w[0], lo[t]) + dot_t(w[1], h)
        for part in range(2):
            for g in range(groups):
                base = (part * groups + g) * each
                for c in range(length // 128):
                    out[g, part, c, pl.ds(t, each, stride=RADIX), :] = got[
                        base : base + each, c * 128 : c * 128 + 128
                    ]
        return carry

    lax.fori_loop(0, RADIX, multiply, 0)


def transform_y(f, twiddle, matrix, groups, each):
    sources, length, width = f.shape
    inner = sources * width // RADIX
    return pl.pallas_call(
        functools.partial(y_kernel, inner, groups, each),
        out_shape=jax.ShapeDtypeStruct((groups, 2, length // 128, each * RADIX, 128), F32),
        in_specs=[pl.BlockSpec(memory_space=pltpu.VMEM)] * 3,
        out_specs=pl.BlockSpec(memory_space=pltpu.VMEM),
        scratch_shapes=[
            pltpu.VMEM((RADIX, length, 2 * inner), BF),
            pltpu.VMEM((RADIX, length, 2 * inner), BF),
        ],
        compiler_params=pltpu.CompilerParams(vmem_limit_bytes=56 * 2**20),
        cost_estimate=pl.CostEstimate(flops=10**11, bytes_accessed=10**7, transcendentals=0),
        name="transform_y",
    )(f, twiddle, matrix)


def x_kernel(z, tw, v, *rest):
    out, hi, lo, wide = rest[-4:]
    count, _, pieces, waves, lanes_each = z.shape
    length = pieces * lanes_each
    inner = wide.shape[1] // count

    def strip(i, carry):
        r = pl.ds(pl.multiple_of(i * 16, 16), 16)
        for c in range(pieces):
            lane = slice(c * lanes_each, (c + 1) * lanes_each)
            values = [(z[a, 0, c, r, :].astype(F32), z[a, 1, c, r, :].astype(F32)) for a in range(count)]
            for t, (re, im) in enumerate(fft(values)):
                cos = tw[0, t : t + 1, lane]
                sin = tw[1, t : t + 1, lane]
                zrh, zrl = split(re * cos + im * sin)
                zih, zil = split(im * cos - re * sin)
                hi[t, r, lane] = zrh
                lo[t, r, lane] = zrl
                lane_i = slice(length + c * lanes_each, length + (c + 1) * lanes_each)
                hi[t, r, lane_i] = zih
                lo[t, r, lane_i] = zil
        return carry

    lax.fori_loop(0, waves // 16, strip, 0)

    def multiply(t, carry):
        h = hi[t]
        got = dot_t(v[0], h) + dot_t(v[0], lo[t]) + dot_t(v[1], h)
        for part in range(2):
            wide[part, pl.ds(t, inner, stride=count), :] = got[part * inner : (part + 1) * inner]
        return carry

    lax.fori_loop(0, count, multiply, 0)

    def turn(c, carry):
        block = pl.ds(pl.multiple_of(c * 256, 256), 256)
        for part in range(2):
            out[part, :, block] = wide[part, block, :].T[: out.shape[1]]
        return carry

    lax.fori_loop(0, wide.shape[1] // 256, turn, 0)


def transform_x(z, twiddle, matrix, level, levels, earlier):
    count, _, pieces, waves, lanes_each = z.shape
    length = pieces * lanes_each
    total = count * length
    padded = max(waves, 128)
    return pl.pallas_call(
        x_kernel,
        out_shape=jax.ShapeDtypeStruct((2, levels, waves, total), F32),
        grid=(1,),
        in_specs=[pl.BlockSpec(memory_space=pltpu.VMEM)] * 3
        + [pl.BlockSpec(memory_space=pl.ANY)] * len(earlier),
        out_specs=pl.BlockSpec((2, None, waves, total), lambda i: (0, level, 0, 0)),
        input_output_aliases={3: 0} if earlier else {},
        scratch_shapes=[
            pltpu.VMEM((count, padded, 2 * length), BF),
            pltpu.VMEM((count, padded, 2 * length), BF),
            pltpu.VMEM((2, total, padded), F32),
        ],
        compiler_params=pltpu.CompilerParams(vmem_limit_bytes=56 * 2**20),
        cost_estimate=pl.CostEstimate(flops=10**11, bytes_accessed=10**7, transcendentals=0),
        name="transform_x",
    )(z, twiddle, matrix, *earlier)


def tables(count_x, count_y, length, width):
    total_x, total_y = count_x * length, count_y * width
    inner = total_y // RADIX
    waves = total_y // (count_x * count_y)
    each = waves // RADIX
    p = np.arange(inner)
    shift = np.arange(RADIX)[None, :, None] + waves * np.arange(count_y)[:, None, None]
    angle = 2 * np.pi * ((shift * p) % total_y) / total_y
    tw_y = np.stack([np.cos(angle), np.sin(angle)], axis=1).astype(np.float32)
    m = ((np.arange(count_x) * count_y * each)[:, None] + np.arange(each)[None, :]).reshape(-1)
    w = complex_matrix(2 * np.pi * ((m[:, None] * p[None, :]) % inner) / inner, 1 / math.sqrt(total_y))
    l = np.arange(length)
    angle = 2 * np.pi * ((np.arange(count_x)[:, None] * l[None, :]) % total_x) / total_x
    tw_x = np.stack([np.cos(angle), np.sin(angle)]).astype(np.float32)
    v = complex_matrix(2 * np.pi * ((l[:, None] * l[None, :]) % length) / length, 1 / math.sqrt(total_x))
    return tw_y, w, tw_x, v, each


def around(axis, first, final):
    count = lax.axis_size(axis)
    up = [(i, (i + 1) % count) for i in range(count)]
    down = [(j, i) for i, j in up]
    return lax.ppermute(final, axis, up), lax.ppermute(first, axis, down)


def body(state, heights, flag):
    _, levels, length, width = state.shape
    count_x, count_y = lax.axis_size("gx"), lax.axis_size("gy")
    tw_y, w, tw_x, v, each = tables(count_x, count_y, length, width)

    def pieces(lo, hi, axis):
        s = lax.slice_in_dim(state, lo, hi, axis=axis + 2)
        s = s.reshape((8,) + s.shape[2:])
        return jnp.concatenate([s, lax.slice_in_dim(heights, lo, hi, axis=axis)[None].astype(BF)], axis=0)

    xlo, xhi = around("gx", pieces(0, 8, 0), pieces(length - 8, length, 0))
    left = jnp.concatenate([xlo[:, :, :4], pieces(0, 4, 1), xhi[:, :, :4]], axis=1)
    right = jnp.concatenate(
        [xlo[:, :, width - 4 :], pieces(width - 4, width, 1), xhi[:, :, width - 4 :]], axis=1
    )
    before, after = around("gy", left, right)
    yl = jnp.pad(before, ((0, 0), (0, 0), (124, 0)))
    yr = jnp.pad(after, ((0, 0), (0, 0), (0, 124)))
    tendency, div0, div1 = stencil(state, heights, flag, xlo, xhi, yl, yr)

    mine = lax.axis_index("gy")
    twiddle = lax.dynamic_index_in_dim(jnp.asarray(tw_y), mine, 0, keepdims=False)
    swap = [(i, 1 - i) for i in range(count_y)]
    earlier = ()
    for level, div in enumerate((div0, div1)):
        own = div.astype(SEND)
        if count_y == 2:
            if level:
                own, other = lax.optimization_barrier((own, other))
            other = lax.ppermute(own, "gy", swap)
            if level:
                _, own, mixed = lax.optimization_barrier((waves, own, other))
            else:
                mixed = other
            lines = jnp.stack([jnp.where(mine == 0, own, mixed), jnp.where(mine == 0, mixed, own)])
        else:
            lines = lax.all_gather(own, "gy", axis=0)
        waves = transform_y(lines.astype(F32), twiddle, jnp.asarray(w), count_x, each)
        moved = lax.all_to_all(waves.astype(SEND), "gx", split_axis=0, concat_axis=0, tiled=True)
        earlier = (
            transform_x(moved.astype(F32), jnp.asarray(tw_x), jnp.asarray(v), level, levels, earlier),
        )
    return tendency, earlier[0]


def solution(mesh):
    return jax.shard_map(
        body,
        mesh=mesh,
        in_specs=(P(None, None, "gx", "gy"), P("gx", "gy"), P("gx", "gy")),
        out_specs=(P(None, None, "gx", "gy"), P(None, None, ("gx", "gy"), None)),
        check_vma=False,
    )
```

```python
import functools
import math

import jax
import jax.numpy as jnp
import numpy as np
from jax import lax
from jax.experimental import pallas as pl
from jax.experimental.pallas import tpu as pltpu
from jax.sharding import PartitionSpec as P

NU = 0.1
BETA = 0.5
HEAT = 1.0
DT = 0.5
RADIX = 16
SEND = jnp.float16
BF = jnp.bfloat16
F32 = jnp.float32
SLOPE = {1: 45.0, -1: -45.0, 2: -9.0, -2: 9.0, 3: 1.0, -3: -1.0}
CURVE_X = {1: 1.0, -1: 1.0}
CURVE_Y = {0: -6.0, 1: 1.0, -1: 1.0}
CENTRAL = {1: 1.0, -1: -1.0}


def band(rows, columns, offset, taps):
    step = np.arange(rows)[:, None] - np.arange(columns)[None, :] - offset
    out = np.zeros((rows, columns), np.float32)
    for key, value in taps.items():
        out[step == key] = value
    return out


def dot(a, b):
    return jnp.dot(a, b, preferred_element_type=F32)


def dot_t(a, b):
    return lax.dot_general(a, b, (((1,), (1,)), ((), ())), preferred_element_type=F32)


def stencil_kernel(
    bx, width,
    main, prev, nxt, heights, h_prev, h_next, flag, xlo, xhi, yl, yr, dy, dx, sy, sx,
    tend, div0, div1,
    m_s, h_s, t_s, every,
):
    i = pl.program_id(0)
    last = pl.num_programs(0) - 1
    rows = bx + 16
    ext = width + 256
    mine = slice(8, 8 + bx)
    divs = (div0, div1)
    side = pl.ds(pl.multiple_of(i * bx, 16), rows)


    piece = 256

    def fill(c, carry):
        lanes = pl.ds(pl.multiple_of(c * piece, 128), piece)
        target = pl.ds(pl.multiple_of(128 + c * piece, 128), piece)

        def edge(field, ref_low, ref_high, middle):
            low = jnp.where(i == 0, xlo[field, :, lanes].astype(F32), ref_low)
            high = jnp.where(i == last, xhi[field, :, lanes].astype(F32), ref_high)
            return jnp.concatenate([low, middle, high], axis=0)

        h = edge(
            8, h_prev[:, lanes].astype(F32), h_next[:, lanes].astype(F32),
            heights[:, lanes].astype(F32),
        )
        h_s[:, target] = h
        for f in range(8):
            value = edge(
                f, prev[f // 2, f % 2, :, lanes].astype(F32)[8:],
                nxt[f // 2, f % 2, :, lanes].astype(F32)[:8],
                main[f // 2, f % 2, :, lanes].astype(F32),
            )
            m_s[f, :, target] = jnp.where(h <= float(f % 2), value, 0.0).astype(BF)
        return carry

    lax.fori_loop(0, width // piece, fill, 0)
    for ref, target in ((yl, slice(0, 128)), (yr, slice(width + 128, ext))):
        h = ref[8, side, :].astype(F32)
        h_s[:, target] = h
        for f in range(8):
            m_s[f, :, target] = jnp.where(
                h <= float(f % 2), ref[f, side, :].astype(F32), 0.0
            ).astype(BF)

    def tendency(f, lanes, along_y, centers, n):
        k = f % 2
        mid = m_s[f, :, lanes]
        along_x = dot(dx[...], mid)
        other = m_s[f + 1 - 2 * k, :, lanes].astype(F32)
        u60, v60, wz = centers[k]
        lap = along_y[:, n:] + along_x[rows:] + other
        out = NU * lap - (u60 * along_x[:rows] + v60 * along_y[:, :n] + wz * other)
        return out

    def centers_of(lanes):
        out = []
        for k in range(2):
            sign = 0.5 if k == 0 else -0.5
            out.append((
                m_s[k, :, lanes].astype(F32) * (1.0 / 60.0),
                m_s[2 + k, :, lanes].astype(F32) * (1.0 / 60.0),
                m_s[4 + k, :, lanes].astype(F32) * sign,
            ))
        return out

    def first(j, carry):
        start = pl.multiple_of(j * 256, 128)
        lanes = pl.ds(pl.multiple_of(start + 128, 128), 256)
        window = pl.ds(start, 512)
        outs = pl.ds(start, 256)
        centers = centers_of(lanes)
        h = h_s[:, lanes]
        fluids = [(h <= float(k)).astype(F32) for k in range(2)]
        shine = flag[:, outs].astype(F32)
        stars = []
        every[...] = dot(m_s[:, :, window].reshape(8 * rows, 512), dy[...])
        for k in range(2):
            for c in (0, 1, 2, 3):
                f = 2 * c + k
                t = tendency(f, lanes, every[f * rows : (f + 1) * rows, :], centers, 256)
                if c == 2:
                    t = t + BETA * m_s[6 + k, :, lanes].astype(F32)
                if c == 3:
                    t = t[mine] + HEAT * jnp.where(h[mine] == float(k), shine, 0.0)
                    tend[c, k, :, outs] = (fluids[k][mine] * t).astype(BF)
                    continue
                t = fluids[k] * t
                tend[c, k, :, outs] = t[mine].astype(BF)
                if c == 0:
                    tb = t.astype(BF)
                    divs[k][:, outs] = dot(sx[0], m_s[f, :, lanes]) + dot(sx[1], tb)
                if c == 1:
                    t_s[k, :, lanes] = t.astype(BF)
                if c == 2:
                    tb = t[mine].astype(BF).astype(F32)
                    stars.append(m_s[f, :, lanes].astype(F32)[mine] + DT * tb)
        div0[:, outs] += stars[1]
        div1[:, outs] -= stars[0]
        return carry

    lax.fori_loop(0, width // 256, first, 0)

    for target, window, matrix in (
        (slice(0, 128), slice(0, 256),
         jnp.concatenate([dy[128:384, 0:128], dy[128:384, 256:384]], axis=1)),
        (slice(ext - 128, ext), slice(ext - 256, ext),
         jnp.concatenate([dy[0:256, 0:128], dy[0:256, 256:384]], axis=1)),
    ):
        centers = centers_of(target)
        h = h_s[:, target]
        for k in range(2):
            t = tendency(2 + k, target, dot(m_s[2 + k, :, window], matrix), centers, 128)
            t_s[k, :, target] = jnp.where(h <= float(k), t, 0.0).astype(BF)

    def second(j, carry):
        start = pl.multiple_of(j * 256, 128)
        window = pl.ds(start, 512)
        outs = pl.ds(start, 256)
        for k in range(2):
            part = dot(m_s[2 + k, :, window], sy[0]) + dot(t_s[k, :, window], sy[1])
            divs[k][:, outs] = (divs[k][:, outs] + part[mine]) * 0.5
        return carry

    lax.fori_loop(0, width // 256, second, 0)


def stencil(state, heights, flag, xlo, xhi, yl, yr):
    _, _, length, width = state.shape
    bx = min(128, length)
    rows = bx + 16
    ext = width + 256
    dy = np.concatenate([band(512, 256, 128, SLOPE), band(512, 256, 128, CURVE_Y)], axis=1)
    dx = np.concatenate([band(rows, rows, 0, SLOPE).T, band(rows, rows, 0, CURVE_X).T], axis=0)
    sy = band(512, 256, 128, CENTRAL)
    sy = np.stack([sy, DT * sy])
    sx = band(rows, bx, 8, CENTRAL).T
    sx = np.stack([sx, DT * sx])
    n16 = length // 16
    n8 = length // 8
    full = lambda *shape: pl.BlockSpec(shape, lambda i: (0,) * len(shape))
    return pl.pallas_call(
        functools.partial(stencil_kernel, bx, width),
        grid=(length // bx,),
        out_shape=(
            jax.ShapeDtypeStruct(state.shape, BF),
            jax.ShapeDtypeStruct((length, width), F32),
            jax.ShapeDtypeStruct((length, width), F32),
        ),
        in_specs=[
            pl.BlockSpec((4, 2, bx, width), lambda i: (0, 0, i, 0)),
            pl.BlockSpec((4, 2, 16, width), lambda i: (0, 0, jnp.maximum(i * (bx // 16) - 1, 0), 0)),
            pl.BlockSpec((4, 2, 16, width), lambda i: (0, 0, jnp.minimum((i + 1) * (bx // 16), n16 - 1), 0)),
            pl.BlockSpec((bx, width), lambda i: (i, 0)),
            pl.BlockSpec((8, width), lambda i: (jnp.maximum(i * (bx // 8) - 1, 0), 0)),
            pl.BlockSpec((8, width), lambda i: (jnp.minimum((i + 1) * (bx // 8), n8 - 1), 0)),
            pl.BlockSpec((bx, width), lambda i: (i, 0)),
            full(9, 8, width),
            full(9, 8, width),
            full(9, length + 16, 128),
            full(9, length + 16, 128),
            full(512, 512),
            full(2 * rows, rows),
            full(2, 512, 256),
            full(2, bx, rows),
        ],
        out_specs=(
            pl.BlockSpec((4, 2, bx, width), lambda i: (0, 0, i, 0)),
            pl.BlockSpec((bx, width), lambda i: (i, 0)),
            pl.BlockSpec((bx, width), lambda i: (i, 0)),
        ),
        scratch_shapes=[
            pltpu.VMEM((8, rows, ext), BF),
            pltpu.VMEM((rows, ext), F32),
            pltpu.VMEM((2, rows, ext), BF),
            pltpu.VMEM((8 * rows, 512), F32),
        ],
        compiler_params=pltpu.CompilerParams(vmem_limit_bytes=56 * 2**20),
        name="stencil",
    )(state, state, state, heights, heights, heights, flag, xlo, xhi, yl, yr,
      jnp.asarray(dy, BF), jnp.asarray(dx, BF), jnp.asarray(sy, BF), jnp.asarray(sx, BF))


def fft(values):
    n = len(values)
    if n == 1:
        return values
    even, odd = fft(values[0::2]), fft(values[1::2])
    out = [None] * n
    for k in range(n // 2):
        er, ei = even[k]
        pr, pi = rotate(odd[k], k, n)
        out[k] = (er + pr, ei + pi)
        out[k + n // 2] = (er - pr, ei - pi)
    return out


def rotate(value, k, n):
    re, im = value
    if k == 0:
        return re, im
    if 4 * k == n:
        return im, -re
    if 8 * k == n:
        root = math.sqrt(0.5)
        return (re + im) * root, (im - re) * root
    if 8 * k == 3 * n:
        root = math.sqrt(0.5)
        return (im - re) * root, -(re + im) * root
    c, s = math.cos(2 * math.pi * k / n), math.sin(2 * math.pi * k / n)
    return re * c + im * s, im * c - re * s


def rfft(values):
    n = len(values)
    if n == 2:
        a, b = values
        return [(a + b, None), (a - b, None)]
    even, odd = rfft(values[0::2]), rfft(values[1::2])
    half = n // 2

    def at(part, k):
        if k <= half // 2:
            return part[k]
        re, im = part[half - k]
        return re, None if im is None else -im

    out = []
    for k in range(half + 1):
        er, ei = at(even, k % half)
        orr, oi = at(odd, k % half)
        if k == half:
            out.append((er - orr, None))
        elif k == 0:
            out.append((er + orr, None))
        elif 4 * k == n:
            out.append((er, -orr))
        else:
            if oi is None:
                c, s = math.cos(2 * math.pi * k / n), math.sin(2 * math.pi * k / n)
                pr, pi = orr * c, -orr * s
            else:
                pr, pi = rotate((orr, oi), k, n)
            out.append((er + pr, pi if ei is None else ei + pi))
    return out


def split(value):
    high = value.astype(BF)
    return high, (value - high.astype(F32)).astype(BF)


def complex_matrix(angle, scale):
    c, s = np.cos(angle) * scale, np.sin(angle) * scale
    full = np.block([[c, s], [-s, c]])
    high = full.astype(np.float32).astype(jnp.bfloat16)
    low = (full - high.astype(np.float64)).astype(jnp.bfloat16)
    return np.concatenate([high, low])


def y_kernel(inner, groups, each, f, tw, w, out, hi, lo):
    sources, length, width = f.shape
    chunks = width // inner

    def strip(i, carry):
        r = pl.ds(pl.multiple_of(i * 16, 16), 16)
        for c in range(inner // 128):
            lane = slice(c * 128, c * 128 + 128)
            values = []
            for q in range(RADIX):
                s, o = q // chunks, (q % chunks) * inner + c * 128
                values.append(f[s, r, o : o + 128].astype(F32))
            spec = rfft(values)
            for t in range(RADIX):
                re, im = spec[t if t <= RADIX // 2 else RADIX - t]
                cos = tw[0, t : t + 1, lane]
                sin = tw[1, t : t + 1, lane]
                if im is None:
                    zr, zi = re * cos, -(re * sin)
                elif t <= RADIX // 2:
                    zr, zi = re * cos + im * sin, im * cos - re * sin
                else:
                    zr, zi = re * cos - im * sin, -(im * cos + re * sin)
                zrh, zrl = split(zr)
                zih, zil = split(zi)
                hi[t, r, lane] = zrh
                lo[t, r, lane] = zrl
                lane_i = slice(inner + c * 128, inner + c * 128 + 128)
                hi[t, r, lane_i] = zih
                lo[t, r, lane_i] = zil
        return carry

    lax.fori_loop(0, length // 16, strip, 0)

    def multiply(t, carry):
        h = hi[t]
        both = dot_t(w[...], h)
        n = w.shape[0] // 2
        got = both[:n] + both[n:] + dot_t(w[:n, :], lo[t])
        for part in range(2):
            for g in range(groups):
                base = (part * groups + g) * each
                for c in range(length // 128):
                    out[g, part, c, pl.ds(t, each, stride=RADIX), :] = got[
                        base : base + each, c * 128 : c * 128 + 128
                    ]
        return carry

    lax.fori_loop(0, RADIX, multiply, 0)


def transform_y(f, twiddle, matrix, groups, each):
    sources, length, width = f.shape
    inner = sources * width // RADIX
    return pl.pallas_call(
        functools.partial(y_kernel, inner, groups, each),
        out_shape=jax.ShapeDtypeStruct((groups, 2, length // 128, each * RADIX, 128), F32),
        in_specs=[pl.BlockSpec(memory_space=pltpu.VMEM)] * 3,
        out_specs=pl.BlockSpec(memory_space=pltpu.VMEM),
        scratch_shapes=[
            pltpu.VMEM((RADIX, length, 2 * inner), BF),
            pltpu.VMEM((RADIX, length, 2 * inner), BF),
        ],
        compiler_params=pltpu.CompilerParams(vmem_limit_bytes=56 * 2**20),
        cost_estimate=pl.CostEstimate(flops=10**11, bytes_accessed=10**7, transcendentals=0),
        name="transform_y",
    )(f, twiddle, matrix)


def x_kernel(z, tw, v, *rest):
    out, hi, lo, wide = rest[-4:]
    count, _, pieces, waves, lanes_each = z.shape
    length = pieces * lanes_each
    inner = wide.shape[1] // count

    def strip(i, carry):
        r = pl.ds(pl.multiple_of(i * 16, 16), 16)
        for c in range(pieces):
            lane = slice(c * lanes_each, (c + 1) * lanes_each)
            values = [(z[a, 0, c, r, :].astype(F32), z[a, 1, c, r, :].astype(F32)) for a in range(count)]
            for t, (re, im) in enumerate(fft(values)):
                cos = tw[0, t : t + 1, lane]
                sin = tw[1, t : t + 1, lane]
                zrh, zrl = split(re * cos + im * sin)
                zih, zil = split(im * cos - re * sin)
                hi[t, r, lane] = zrh
                lo[t, r, lane] = zrl
                lane_i = slice(length + c * lanes_each, length + (c + 1) * lanes_each)
                hi[t, r, lane_i] = zih
                lo[t, r, lane_i] = zil
        return carry

    lax.fori_loop(0, waves // 16, strip, 0)

    def multiply(t, carry):
        h = hi[t]
        both = dot_t(v[...], h)
        n = v.shape[0] // 2
        got = both[:n] + both[n:] + dot_t(v[:n, :], lo[t])
        for part in range(2):
            wide[part, pl.ds(t, inner, stride=count), :] = got[part * inner : (part + 1) * inner]
        return carry

    lax.fori_loop(0, count, multiply, 0)

    def turn(c, carry):
        block = pl.ds(pl.multiple_of(c * 256, 256), 256)
        for part in range(2):
            out[part, :, block] = wide[part, block, :].T[: out.shape[1]]
        return carry

    lax.fori_loop(0, wide.shape[1] // 256, turn, 0)


def transform_x(z, twiddle, matrix, level, levels, earlier):
    count, _, pieces, waves, lanes_each = z.shape
    length = pieces * lanes_each
    total = count * length
    padded = max(waves, 128)
    return pl.pallas_call(
        x_kernel,
        out_shape=jax.ShapeDtypeStruct((2, levels, waves, total), F32),
        grid=(1,),
        in_specs=[pl.BlockSpec(memory_space=pltpu.VMEM)] * 3
        + [pl.BlockSpec(memory_space=pl.ANY)] * len(earlier),
        out_specs=pl.BlockSpec((2, None, waves, total), lambda i: (0, level, 0, 0)),
        input_output_aliases={3: 0} if earlier else {},
        scratch_shapes=[
            pltpu.VMEM((count, padded, 2 * length), BF),
            pltpu.VMEM((count, padded, 2 * length), BF),
            pltpu.VMEM((2, total, padded), F32),
        ],
        compiler_params=pltpu.CompilerParams(vmem_limit_bytes=56 * 2**20),
        cost_estimate=pl.CostEstimate(flops=10**11, bytes_accessed=10**7, transcendentals=0),
        name="transform_x",
    )(z, twiddle, matrix, *earlier)


def tables(count_x, count_y, length, width):
    total_x, total_y = count_x * length, count_y * width
    inner = total_y // RADIX
    waves = total_y // (count_x * count_y)
    each = waves // RADIX
    p = np.arange(inner)
    shift = np.arange(RADIX)[None, :, None] + waves * np.arange(count_y)[:, None, None]
    angle = 2 * np.pi * ((shift * p) % total_y) / total_y
    tw_y = np.stack([np.cos(angle), np.sin(angle)], axis=1).astype(np.float32)
    m = ((np.arange(count_x) * count_y * each)[:, None] + np.arange(each)[None, :]).reshape(-1)
    w = complex_matrix(2 * np.pi * ((m[:, None] * p[None, :]) % inner) / inner, 1 / math.sqrt(total_y))
    l = np.arange(length)
    angle = 2 * np.pi * ((np.arange(count_x)[:, None] * l[None, :]) % total_x) / total_x
    tw_x = np.stack([np.cos(angle), np.sin(angle)]).astype(np.float32)
    v = complex_matrix(2 * np.pi * ((l[:, None] * l[None, :]) % length) / length, 1 / math.sqrt(total_x))
    return tw_y, w, tw_x, v, each


def around(axis, first, final):
    count = lax.axis_size(axis)
    up = [(i, (i + 1) % count) for i in range(count)]
    down = [(j, i) for i, j in up]
    return lax.ppermute(final, axis, up), lax.ppermute(first, axis, down)


def body(state, heights, flag):
    _, levels, length, width = state.shape
    count_x, count_y = lax.axis_size("gx"), lax.axis_size("gy")
    tw_y, w, tw_x, v, each = tables(count_x, count_y, length, width)

    def pieces(lo, hi, axis):
        s = lax.slice_in_dim(state, lo, hi, axis=axis + 2)
        s = s.reshape((8,) + s.shape[2:])
        return jnp.concatenate([s, lax.slice_in_dim(heights, lo, hi, axis=axis)[None].astype(BF)], axis=0)

    xlo, xhi = around("gx", pieces(0, 8, 0), pieces(length - 8, length, 0))
    left = jnp.concatenate([xlo[:, :, :4], pieces(0, 4, 1), xhi[:, :, :4]], axis=1)
    right = jnp.concatenate(
        [xlo[:, :, width - 4 :], pieces(width - 4, width, 1), xhi[:, :, width - 4 :]], axis=1
    )
    before, after = around("gy", left, right)
    yl = jnp.pad(before, ((0, 0), (0, 0), (124, 0)))
    yr = jnp.pad(after, ((0, 0), (0, 0), (0, 124)))
    tendency, div0, div1 = stencil(state, heights, flag, xlo, xhi, yl, yr)

    mine = lax.axis_index("gy")
    twiddle = lax.dynamic_index_in_dim(jnp.asarray(tw_y), mine, 0, keepdims=False)
    swap = [(i, 1 - i) for i in range(count_y)]
    earlier = ()
    for level, div in enumerate((div0, div1)):
        own = div.astype(SEND)
        if count_y == 2:
            if level:
                own, other = lax.optimization_barrier((own, other))
            other = lax.ppermute(own, "gy", swap)
            if level:
                _, own, mixed = lax.optimization_barrier((waves, own, other))
            else:
                mixed = other
            lines = jnp.stack([jnp.where(mine == 0, own, mixed), jnp.where(mine == 0, mixed, own)])
        else:
            lines = lax.all_gather(own, "gy", axis=0)
        waves = transform_y(lines.astype(F32), twiddle, jnp.asarray(w), count_x, each)
        moved = lax.all_to_all(waves.astype(SEND), "gx", split_axis=0, concat_axis=0, tiled=True)
        earlier = (
            transform_x(moved.astype(F32), jnp.asarray(tw_x), jnp.asarray(v), level, levels, earlier),
        )
    return tendency, earlier[0]


def solution(mesh):
    return jax.shard_map(
        body,
        mesh=mesh,
        in_specs=(P(None, None, "gx", "gy"), P("gx", "gy"), P("gx", "gy")),
        out_specs=(P(None, None, "gx", "gy"), P(None, None, ("gx", "gy"), None)),
        check_vma=False,
    )
```

```python
import functools
import math

import jax
import jax.numpy as jnp
import numpy as np
from jax import lax
from jax.experimental import pallas as pl
from jax.experimental.pallas import tpu as pltpu
from jax.sharding import PartitionSpec as P

NU = 0.1
BETA = 0.5
HEAT = 1.0
DT = 0.5
RADIX = 16
SEND = jnp.float16
BF = jnp.bfloat16
F32 = jnp.float32
SLOPE = {1: 45.0, -1: -45.0, 2: -9.0, -2: 9.0, 3: 1.0, -3: -1.0}
CURVE_X = {1: 1.0, -1: 1.0}
CURVE_Y = {0: -6.0, 1: 1.0, -1: 1.0}
CENTRAL = {1: 1.0, -1: -1.0}


def band(rows, columns, offset, taps):
    step = np.arange(rows)[:, None] - np.arange(columns)[None, :] - offset
    out = np.zeros((rows, columns), np.float32)
    for key, value in taps.items():
        out[step == key] = value
    return out


def dot(a, b):
    return jnp.dot(a, b, preferred_element_type=F32)


def dot_t(a, b):
    return lax.dot_general(a, b, (((1,), (1,)), ((), ())), preferred_element_type=F32)


def stencil_kernel(
    bx, width,
    main, prev, nxt, heights, h_prev, h_next, flag, xlo, xhi, yl, yr, dy, dx, sy, sx,
    tend, div0, div1,
    m_s, h_s, t_s, every,
):
    i = pl.program_id(0)
    last = pl.num_programs(0) - 1
    rows = bx + 16
    ext = width + 256
    mine = slice(8, 8 + bx)
    divs = (div0, div1)
    side = pl.ds(pl.multiple_of(i * bx, 16), rows)


    piece = 256

    def fill(c, carry):
        lanes = pl.ds(pl.multiple_of(c * piece, 128), piece)
        target = pl.ds(pl.multiple_of(128 + c * piece, 128), piece)

        def edge(field, ref_low, ref_high, middle):
            low = jnp.where(i == 0, xlo[field, :, lanes].astype(F32), ref_low)
            high = jnp.where(i == last, xhi[field, :, lanes].astype(F32), ref_high)
            return jnp.concatenate([low, middle, high], axis=0)

        h = edge(
            8, h_prev[:, lanes].astype(F32), h_next[:, lanes].astype(F32),
            heights[:, lanes].astype(F32),
        )
        h_s[:, target] = h
        for f in range(8):
            value = edge(
                f, prev[f // 2, f % 2, :, lanes].astype(F32)[8:],
                nxt[f // 2, f % 2, :, lanes].astype(F32)[:8],
                main[f // 2, f % 2, :, lanes].astype(F32),
            )
            m_s[f, :, target] = jnp.where(h <= float(f % 2), value, 0.0).astype(BF)
        return carry

    lax.fori_loop(0, width // piece, fill, 0)
    for ref, target in ((yl, slice(0, 128)), (yr, slice(width + 128, ext))):
        h = ref[8, side, :].astype(F32)
        h_s[:, target] = h
        for f in range(8):
            m_s[f, :, target] = jnp.where(
                h <= float(f % 2), ref[f, side, :].astype(F32), 0.0
            ).astype(BF)

    def tendency(f, lanes, along_y, centers, n):
        k = f % 2
        mid = m_s[f, :, lanes]
        along_x = dot(dx[...], mid)
        other = m_s[f + 1 - 2 * k, :, lanes].astype(F32)
        u60, v60, wz = centers[k]
        lap = along_y[:, n:] + along_x[rows:] + other
        out = NU * lap - (u60 * along_x[:rows] + v60 * along_y[:, :n] + wz * other)
        return out

    def centers_of(lanes):
        out = []
        for k in range(2):
            sign = 0.5 if k == 0 else -0.5
            out.append((
                m_s[k, :, lanes].astype(F32) * (1.0 / 60.0),
                m_s[2 + k, :, lanes].astype(F32) * (1.0 / 60.0),
                m_s[4 + k, :, lanes].astype(F32) * sign,
            ))
        return out

    def first(j, carry):
        start = pl.multiple_of(j * 256, 128)
        lanes = pl.ds(pl.multiple_of(start + 128, 128), 256)
        window = pl.ds(start, 512)
        outs = pl.ds(start, 256)
        centers = centers_of(lanes)
        h = h_s[:, lanes]
        fluids = [(h <= float(k)).astype(F32) for k in range(2)]
        shine = flag[:, outs].astype(F32)
        stars = []
        every[...] = dot(m_s[:, :, window].reshape(8 * rows, 512), dy[...])
        for k in range(2):
            for c in (0, 1, 2, 3):
                f = 2 * c + k
                t = tendency(f, lanes, every[f * rows : (f + 1) * rows, :], centers, 256)
                if c == 2:
                    t = t + BETA * m_s[6 + k, :, lanes].astype(F32)
                if c == 3:
                    t = t[mine] + HEAT * jnp.where(h[mine] == float(k), shine, 0.0)
                    tend[c, k, :, outs] = (fluids[k][mine] * t).astype(BF)
                    continue
                t = fluids[k] * t
                tend[c, k, :, outs] = t[mine].astype(BF)
                if c == 0:
                    tb = t.astype(BF)
                    divs[k][:, outs] = dot(sx[0], m_s[f, :, lanes]) + dot(sx[1], tb)
                if c == 1:
                    t_s[k, :, lanes] = t.astype(BF)
                if c == 2:
                    tb = t[mine].astype(BF).astype(F32)
                    stars.append(m_s[f, :, lanes].astype(F32)[mine] + DT * tb)
        div0[:, outs] += stars[1]
        div1[:, outs] -= stars[0]
        return carry

    lax.fori_loop(0, width // 256, first, 0)

    for target, window, matrix in (
        (slice(0, 128), slice(0, 256),
         jnp.concatenate([dy[128:384, 0:128], dy[128:384, 256:384]], axis=1)),
        (slice(ext - 128, ext), slice(ext - 256, ext),
         jnp.concatenate([dy[0:256, 0:128], dy[0:256, 256:384]], axis=1)),
    ):
        centers = centers_of(target)
        h = h_s[:, target]
        for k in range(2):
            t = tendency(2 + k, target, dot(m_s[2 + k, :, window], matrix), centers, 128)
            t_s[k, :, target] = jnp.where(h <= float(k), t, 0.0).astype(BF)

    def second(j, carry):
        start = pl.multiple_of(j * 256, 128)
        window = pl.ds(start, 512)
        outs = pl.ds(start, 256)
        for k in range(2):
            part = dot(m_s[2 + k, :, window], sy[0]) + dot(t_s[k, :, window], sy[1])
            divs[k][:, outs] = (divs[k][:, outs] + part[mine]) * 0.5
        return carry

    lax.fori_loop(0, width // 256, second, 0, unroll=2)


def stencil(state, heights, flag, xlo, xhi, yl, yr):
    _, _, length, width = state.shape
    bx = min(128, length)
    rows = bx + 16
    ext = width + 256
    dy = np.concatenate([band(512, 256, 128, SLOPE), band(512, 256, 128, CURVE_Y)], axis=1)
    dx = np.concatenate([band(rows, rows, 0, SLOPE).T, band(rows, rows, 0, CURVE_X).T], axis=0)
    sy = band(512, 256, 128, CENTRAL)
    sy = np.stack([sy, DT * sy])
    sx = band(rows, bx, 8, CENTRAL).T
    sx = np.stack([sx, DT * sx])
    n16 = length // 16
    n8 = length // 8
    full = lambda *shape: pl.BlockSpec(shape, lambda i: (0,) * len(shape))
    return pl.pallas_call(
        functools.partial(stencil_kernel, bx, width),
        grid=(length // bx,),
        out_shape=(
            jax.ShapeDtypeStruct(state.shape, BF),
            jax.ShapeDtypeStruct((length, width), F32),
            jax.ShapeDtypeStruct((length, width), F32),
        ),
        in_specs=[
            pl.BlockSpec((4, 2, bx, width), lambda i: (0, 0, i, 0)),
            pl.BlockSpec((4, 2, 16, width), lambda i: (0, 0, jnp.maximum(i * (bx // 16) - 1, 0), 0)),
            pl.BlockSpec((4, 2, 16, width), lambda i: (0, 0, jnp.minimum((i + 1) * (bx // 16), n16 - 1), 0)),
            pl.BlockSpec((bx, width), lambda i: (i, 0)),
            pl.BlockSpec((8, width), lambda i: (jnp.maximum(i * (bx // 8) - 1, 0), 0)),
            pl.BlockSpec((8, width), lambda i: (jnp.minimum((i + 1) * (bx // 8), n8 - 1), 0)),
            pl.BlockSpec((bx, width), lambda i: (i, 0)),
            full(9, 8, width),
            full(9, 8, width),
            full(9, length + 16, 128),
            full(9, length + 16, 128),
            full(512, 512),
            full(2 * rows, rows),
            full(2, 512, 256),
            full(2, bx, rows),
        ],
        out_specs=(
            pl.BlockSpec((4, 2, bx, width), lambda i: (0, 0, i, 0)),
            pl.BlockSpec((bx, width), lambda i: (i, 0)),
            pl.BlockSpec((bx, width), lambda i: (i, 0)),
        ),
        scratch_shapes=[
            pltpu.VMEM((8, rows, ext), BF),
            pltpu.VMEM((rows, ext), F32),
            pltpu.VMEM((2, rows, ext), BF),
            pltpu.VMEM((8 * rows, 512), F32),
        ],
        compiler_params=pltpu.CompilerParams(vmem_limit_bytes=56 * 2**20),
        name="stencil",
    )(state, state, state, heights, heights, heights, flag, xlo, xhi, yl, yr,
      jnp.asarray(dy, BF), jnp.asarray(dx, BF), jnp.asarray(sy, BF), jnp.asarray(sx, BF))


def fft(values):
    n = len(values)
    if n == 1:
        return values
    even, odd = fft(values[0::2]), fft(values[1::2])
    out = [None] * n
    for k in range(n // 2):
        er, ei = even[k]
        pr, pi = rotate(odd[k], k, n)
        out[k] = (er + pr, ei + pi)
        out[k + n // 2] = (er - pr, ei - pi)
    return out


def rotate(value, k, n):
    re, im = value
    if k == 0:
        return re, im
    if 4 * k == n:
        return im, -re
    if 8 * k == n:
        root = math.sqrt(0.5)
        return (re + im) * root, (im - re) * root
    if 8 * k == 3 * n:
        root = math.sqrt(0.5)
        return (im - re) * root, -(re + im) * root
    c, s = math.cos(2 * math.pi * k / n), math.sin(2 * math.pi * k / n)
    return re * c + im * s, im * c - re * s


def rfft(values):
    n = len(values)
    if n == 2:
        a, b = values
        return [(a + b, None), (a - b, None)]
    even, odd = rfft(values[0::2]), rfft(values[1::2])
    half = n // 2

    def at(part, k):
        if k <= half // 2:
            return part[k]
        re, im = part[half - k]
        return re, None if im is None else -im

    out = []
    for k in range(half + 1):
        er, ei = at(even, k % half)
        orr, oi = at(odd, k % half)
        if k == half:
            out.append((er - orr, None))
        elif k == 0:
            out.append((er + orr, None))
        elif 4 * k == n:
            out.append((er, -orr))
        else:
            if oi is None:
                c, s = math.cos(2 * math.pi * k / n), math.sin(2 * math.pi * k / n)
                pr, pi = orr * c, -orr * s
            else:
                pr, pi = rotate((orr, oi), k, n)
            out.append((er + pr, pi if ei is None else ei + pi))
    return out


def split(value):
    high = value.astype(BF)
    return high, (value - high.astype(F32)).astype(BF)


def complex_matrix(angle, scale):
    c, s = np.cos(angle) * scale, np.sin(angle) * scale
    full = np.block([[c, s], [-s, c]])
    high = full.astype(np.float32).astype(jnp.bfloat16)
    low = (full - high.astype(np.float64)).astype(jnp.bfloat16)
    return np.concatenate([high, low])


def y_kernel(inner, groups, each, f, tw, w, out, hi, lo):
    sources, length, width = f.shape
    chunks = width // inner

    def strip(i, carry):
        r = pl.ds(pl.multiple_of(i * 16, 16), 16)
        for c in range(inner // 128):
            lane = slice(c * 128, c * 128 + 128)
            values = []
            for q in range(RADIX):
                s, o = q // chunks, (q % chunks) * inner + c * 128
                values.append(f[s, r, o : o + 128].astype(F32))
            spec = rfft(values)
            for t in range(RADIX):
                re, im = spec[t if t <= RADIX // 2 else RADIX - t]
                cos = tw[0, t : t + 1, lane]
                sin = tw[1, t : t + 1, lane]
                if im is None:
                    zr, zi = re * cos, -(re * sin)
                elif t <= RADIX // 2:
                    zr, zi = re * cos + im * sin, im * cos - re * sin
                else:
                    zr, zi = re * cos - im * sin, -(im * cos + re * sin)
                zrh, zrl = split(zr)
                zih, zil = split(zi)
                hi[t, r, lane] = zrh
                lo[t, r, lane] = zrl
                lane_i = slice(inner + c * 128, inner + c * 128 + 128)
                hi[t, r, lane_i] = zih
                lo[t, r, lane_i] = zil
        return carry

    lax.fori_loop(0, length // 16, strip, 0)

    def multiply(t, carry):
        h = hi[t]
        both = dot_t(w[...], h)
        n = w.shape[0] // 2
        got = both[:n] + both[n:] + dot_t(w[:n, :], lo[t])
        for part in range(2):
            for g in range(groups):
                base = (part * groups + g) * each
                for c in range(length // 128):
                    out[g, part, c, pl.ds(t, each, stride=RADIX), :] = got[
                        base : base + each, c * 128 : c * 128 + 128
                    ]
        return carry

    lax.fori_loop(0, RADIX, multiply, 0, unroll=4)


def transform_y(f, twiddle, matrix, groups, each):
    sources, length, width = f.shape
    inner = sources * width // RADIX
    return pl.pallas_call(
        functools.partial(y_kernel, inner, groups, each),
        out_shape=jax.ShapeDtypeStruct((groups, 2, length // 128, each * RADIX, 128), F32),
        in_specs=[pl.BlockSpec(memory_space=pltpu.VMEM)] * 3,
        out_specs=pl.BlockSpec(memory_space=pltpu.VMEM),
        scratch_shapes=[
            pltpu.VMEM((RADIX, length, 2 * inner), BF),
            pltpu.VMEM((RADIX, length, 2 * inner), BF),
        ],
        compiler_params=pltpu.CompilerParams(vmem_limit_bytes=56 * 2**20),
        cost_estimate=pl.CostEstimate(flops=10**11, bytes_accessed=10**7, transcendentals=0),
        name="transform_y",
    )(f, twiddle, matrix)


def x_kernel(z, tw, v, *rest):
    out, hi, lo, wide = rest[-4:]
    count, _, pieces, waves, lanes_each = z.shape
    length = pieces * lanes_each
    inner = wide.shape[1] // count

    def strip(i, carry):
        r = pl.ds(pl.multiple_of(i * 16, 16), 16)
        for c in range(pieces):
            lane = slice(c * lanes_each, (c + 1) * lanes_each)
            values = [(z[a, 0, c, r, :].astype(F32), z[a, 1, c, r, :].astype(F32)) for a in range(count)]
            for t, (re, im) in enumerate(fft(values)):
                cos = tw[0, t : t + 1, lane]
                sin = tw[1, t : t + 1, lane]
                zrh, zrl = split(re * cos + im * sin)
                zih, zil = split(im * cos - re * sin)
                hi[t, r, lane] = zrh
                lo[t, r, lane] = zrl
                lane_i = slice(length + c * lanes_each, length + (c + 1) * lanes_each)
                hi[t, r, lane_i] = zih
                lo[t, r, lane_i] = zil
        return carry

    lax.fori_loop(0, waves // 16, strip, 0)

    def multiply(t, carry):
        h = hi[t]
        both = dot_t(v[...], h)
        n = v.shape[0] // 2
        got = both[:n] + both[n:] + dot_t(v[:n, :], lo[t])
        for part in range(2):
            wide[part, pl.ds(t, inner, stride=count), :] = got[part * inner : (part + 1) * inner]
        return carry

    lax.fori_loop(0, count, multiply, 0, unroll=4)

    def turn(c, carry):
        block = pl.ds(pl.multiple_of(c * 256, 256), 256)
        for part in range(2):
            out[part, :, block] = wide[part, block, :].T[: out.shape[1]]
        return carry

    lax.fori_loop(0, wide.shape[1] // 256, turn, 0, unroll=4)


def transform_x(z, twiddle, matrix, level, levels, earlier):
    count, _, pieces, waves, lanes_each = z.shape
    length = pieces * lanes_each
    total = count * length
    padded = max(waves, 128)
    return pl.pallas_call(
        x_kernel,
        out_shape=jax.ShapeDtypeStruct((2, levels, waves, total), F32),
        grid=(1,),
        in_specs=[pl.BlockSpec(memory_space=pltpu.VMEM)] * 3
        + [pl.BlockSpec(memory_space=pl.ANY)] * len(earlier),
        out_specs=pl.BlockSpec((2, None, waves, total), lambda i: (0, level, 0, 0)),
        input_output_aliases={3: 0} if earlier else {},
        scratch_shapes=[
            pltpu.VMEM((count, padded, 2 * length), BF),
            pltpu.VMEM((count, padded, 2 * length), BF),
            pltpu.VMEM((2, total, padded), F32),
        ],
        compiler_params=pltpu.CompilerParams(vmem_limit_bytes=56 * 2**20),
        cost_estimate=pl.CostEstimate(flops=10**11, bytes_accessed=10**7, transcendentals=0),
        name="transform_x",
    )(z, twiddle, matrix, *earlier)


def tables(count_x, count_y, length, width):
    total_x, total_y = count_x * length, count_y * width
    inner = total_y // RADIX
    waves = total_y // (count_x * count_y)
    each = waves // RADIX
    p = np.arange(inner)
    shift = np.arange(RADIX)[None, :, None] + waves * np.arange(count_y)[:, None, None]
    angle = 2 * np.pi * ((shift * p) % total_y) / total_y
    tw_y = np.stack([np.cos(angle), np.sin(angle)], axis=1).astype(np.float32)
    m = ((np.arange(count_x) * count_y * each)[:, None] + np.arange(each)[None, :]).reshape(-1)
    w = complex_matrix(2 * np.pi * ((m[:, None] * p[None, :]) % inner) / inner, 1 / math.sqrt(total_y))
    l = np.arange(length)
    angle = 2 * np.pi * ((np.arange(count_x)[:, None] * l[None, :]) % total_x) / total_x
    tw_x = np.stack([np.cos(angle), np.sin(angle)]).astype(np.float32)
    v = complex_matrix(2 * np.pi * ((l[:, None] * l[None, :]) % length) / length, 1 / math.sqrt(total_x))
    return tw_y, w, tw_x, v, each


def around(axis, first, final):
    count = lax.axis_size(axis)
    up = [(i, (i + 1) % count) for i in range(count)]
    down = [(j, i) for i, j in up]
    return lax.ppermute(final, axis, up), lax.ppermute(first, axis, down)


def body(state, heights, flag):
    _, levels, length, width = state.shape
    count_x, count_y = lax.axis_size("gx"), lax.axis_size("gy")
    tw_y, w, tw_x, v, each = tables(count_x, count_y, length, width)

    def pieces(lo, hi, axis):
        s = lax.slice_in_dim(state, lo, hi, axis=axis + 2)
        s = s.reshape((8,) + s.shape[2:])
        return jnp.concatenate([s, lax.slice_in_dim(heights, lo, hi, axis=axis)[None].astype(BF)], axis=0)

    xlo, xhi = around("gx", pieces(0, 8, 0), pieces(length - 8, length, 0))
    left = jnp.concatenate([xlo[:, :, :4], pieces(0, 4, 1), xhi[:, :, :4]], axis=1)
    right = jnp.concatenate(
        [xlo[:, :, width - 4 :], pieces(width - 4, width, 1), xhi[:, :, width - 4 :]], axis=1
    )
    before, after = around("gy", left, right)
    yl = jnp.pad(before, ((0, 0), (0, 0), (124, 0)))
    yr = jnp.pad(after, ((0, 0), (0, 0), (0, 124)))
    tendency, div0, div1 = stencil(state, heights, flag, xlo, xhi, yl, yr)

    mine = lax.axis_index("gy")
    twiddle = lax.dynamic_index_in_dim(jnp.asarray(tw_y), mine, 0, keepdims=False)
    swap = [(i, 1 - i) for i in range(count_y)]
    earlier = ()
    for level, div in enumerate((div0, div1)):
        own = div.astype(SEND)
        if count_y == 2:
            if level:
                own, other = lax.optimization_barrier((own, other))
            other = lax.ppermute(own, "gy", swap)
            if level:
                _, own, mixed = lax.optimization_barrier((waves, own, other))
            else:
                mixed = other
            lines = jnp.stack([jnp.where(mine == 0, own, mixed), jnp.where(mine == 0, mixed, own)])
        else:
            lines = lax.all_gather(own, "gy", axis=0)
        waves = transform_y(lines.astype(F32), twiddle, jnp.asarray(w), count_x, each)
        moved = lax.all_to_all(waves.astype(SEND), "gx", split_axis=0, concat_axis=0, tiled=True)
        earlier = (
            transform_x(moved.astype(F32), jnp.asarray(tw_x), jnp.asarray(v), level, levels, earlier),
        )
    return tendency, earlier[0]


def solution(mesh):
    return jax.shard_map(
        body,
        mesh=mesh,
        in_specs=(P(None, None, "gx", "gy"), P("gx", "gy"), P("gx", "gy")),
        out_specs=(P(None, None, "gx", "gy"), P(None, None, ("gx", "gy"), None)),
        check_vma=False,
    )
```
